32 devices in a mesh: req: 4 (over z), blk: 8 (over y, x, core).
Axes of the slice: x: 2, y: 2, z: 4, core: 2. Of those that a mesh axis runs over, the one named last changes fastest.
Arguments:
- queries: bfloat16 [4, 2048, 2048], P('req', 'blk'), may hold values from -6 to 6
- span_keys: bfloat16 [4, 2048, 512], P('req', 'blk'), may hold values from -6 to 6
- span_values: bfloat16 [4, 2048, 512], P('req', 'blk'), may hold values from -6 to 6
- cache_keys: bfloat16 [4, 4096, 512], P('req', 'blk'), may hold values from -6 to 6
- cache_values: bfloat16 [4, 4096, 512], P('req', 'blk'), may hold values from -6 to 6
- lengths: int32 [4], P('req'), may hold values from 1 to 4096, 10240 in all
- inputs: bfloat16 [4, 2048, 2048], P('req', 'blk'), may hold values from -0.59765625 to 0.59765625
- w_out: bfloat16 [2048, 2048], replicated, may hold values from -0.125 to 0.125
- norm_gain: float32 [2048], replicated, may hold values from 0.1 to 1.9
- route_ids: int32 [4, 2048, 6], P('req', 'blk'), may hold values from 0 to 63, all different within a row; in each aligned block of 256 rows (0 to 255, 256 to 511, ..., all dimensions but the last counted through in order) at most 48 rows name the same one
- route_weights: float32 [4, 2048, 6], P('req', 'blk'), may hold values from 0.2 to 1
- w_gate_up: bfloat16 [128, 1408, 2048], P(('req', 'blk')), may hold values from -0.125 to 0.125
- w_down: bfloat16 [128, 704, 2048], P(('req', 'blk')), may hold values from -0.15625 to 0.15625
Outputs:
- outputs: bfloat16 [4, 2048, 2048], P('req', 'blk')
The draws below stay inside these ranges and needn't reach their ends.
Inputs may be any that keep to these rules, and one draw needn't show every extreme that they name: `lengths`: the longest cache is exactly 4096. `route_ids`: A token names 6 different experts; within the rows of one device (aligned blocks of 256 tokens) no expert is named more than 48 times, a bound that some block reaches.
All inputs are finite; a program needn't handle non-finite values. No bound on the sum of `lengths` on one device may be relied on, other than what follows from the above.
Results may differ from the reference program's by a relative error of at most 0.019.
Values may be sent and summed in bfloat16 or wider, within the bound.
A program may use at most 256 MiB of HBM per device.

```python
import math
import jax
import jax.numpy as jnp
import numpy as np
from jax import lax

D = 2048
HEADS = 16
KV_HEADS = 4
HEAD_DIM = 128
FF_E = 1408
EXPERTS = 64
TOP = 6
SPAN = 2048
CTX = 4096
REQS = 4
TOK_DEV = 256
HALF = 704
CAP = 48
N_BLK = 8


def draw_queries(key, part):
    full_shape = (REQS, SPAN, HEADS * HEAD_DIM)
    return (1.4 * jax.random.truncated_normal(jax.random.fold_in(key, 1), -4.0, 4.0, full_shape, jnp.float32)).astype(jnp.bfloat16)


def draw_span_keys(key, part):
    full_shape = (REQS, SPAN, KV_HEADS * HEAD_DIM)
    return jax.random.truncated_normal(jax.random.fold_in(key, 2), -4.0, 4.0, full_shape, jnp.float32).astype(jnp.bfloat16)


def levels(own_key, extent, shards, least, largest):
    level, own = 1.0, jax.random.fold_in(own_key, 6)
    for position, shards_of in shards:
        steps = jnp.exp(jax.random.uniform(jax.random.fold_in(own, position), (shards_of,), jnp.float32, least / len(shards), largest / len(shards)))
        level = level * jnp.repeat(steps, extent[position] // shards_of).reshape([-1 if axis == position else 1 for axis in range(len(extent))])
    return level


def length_profile(count, total, limit, lean):
    weights = [(1 << 20) // math.isqrt(standing ** lean) + 1 for standing in range(2, count + 1)]
    surplus, counts = total - limit - (count - 1), [1] * (count - 1)
    while surplus > 0:
        free = [i for i in range(count - 1) if counts[i] < limit]
        mass, left = sum([weights[i] for i in free]), surplus
        for i in free:
            extra = min(limit - counts[i], max(1, left * weights[i] // mass), surplus)
            counts[i] = counts[i] + extra
            surplus = surplus - extra
    return np.array([limit] + counts)


def ragged(stream_key, count, total, reach, skew):
    if count == 2:
        one = jax.random.randint(stream_key, (), max(1, total - reach), min(reach, total - 1) + 1)
        return jnp.stack([one, total - one])
    sizes = jnp.asarray(length_profile(count, total, reach, skew), jnp.int32)
    couples = (count - 1) // 2
    donor, taker = sizes[1:1 + 2 * couples:2], sizes[2:2 + 2 * couples:2]
    slack = jnp.minimum(donor - 1, reach - taker)
    shifted = jax.random.randint(jax.random.fold_in(stream_key, 1), (couples,), 0, 1 << 20) % (slack + 1)
    sizes = sizes.at[1:1 + 2 * couples:2].set(donor - shifted).at[2:2 + 2 * couples:2].set(taker + shifted)
    return sizes[jax.random.permutation(jax.random.fold_in(stream_key, 2), count)]


def routed_block(key, own, number, rows, amount, top, limit, slope):
    sequence = jax.random.permutation(key, amount)
    crowded, usual = shares(amount, rows * top, limit, slope, True), shares(amount, rows * top, limit, slope, False)
    places = jnp.arange(amount)

    def named(sizes, turn):
        used = int((sizes > 0).sum())
        fixed = max(1, used // 4)
        shifted = fixed + (places - fixed + turn * (used - fixed)) % max(1, amount - fixed)
        return jnp.zeros((amount,), jnp.int32).at[sequence[jnp.where(places < fixed, places, shifted)]].set(jnp.asarray(sizes, jnp.int32))

    sizes = jnp.where(number % 4 == 0, named(crowded, number // 4), named(usual, number - number // 4 - 1))
    mixed = jax.random.permutation(jax.random.fold_in(own, 3), amount)
    giver, sink = mixed[0:amount // 2 * 2:2], mixed[1:amount // 2 * 2:2]
    margin = jnp.minimum(sizes[giver] - 1, limit - sizes[sink]) // 2
    margin = jnp.where((giver == sequence[0]) | (sink == sequence[0]) | (sizes[sink] == 0), 0, jnp.maximum(margin, 0))
    shifted = jax.random.randint(jax.random.fold_in(own, 4), (amount // 2,), 0, 1 << 20) % (margin + 1)
    sizes = sizes.at[giver].add(-shifted).at[sink].add(shifted)
    items = jnp.searchsorted(jnp.cumsum(sizes), jnp.arange(rows * top), side="right").astype(jnp.int32)
    table = items.reshape(top, rows).T
    table = table[jax.random.permutation(jax.random.fold_in(own, 1), rows)]
    turn = jax.random.randint(jax.random.fold_in(own, 2), (rows, 1), 0, top)
    return jnp.take_along_axis(table, (jnp.arange(top)[None, :] + turn) % top, axis=1)


def shares(number_of, total, bound, lean, full):
    loads = [(1 << 20) // math.isqrt(standing ** lean) + 1 for standing in range(1, number_of + 1)]
    largest = bound if full else min(bound, max(-(-total // number_of), total * loads[0] // sum(loads)))
    least = 1 if total - largest >= number_of - 1 else 0
    given, rest = [largest] + [least] * (number_of - 1), total - largest - least * (number_of - 1)
    while rest > 0:
        free = [i for i in range(1, number_of) if given[i] < largest] or [i for i in range(1, number_of) if given[i] < bound]
        mass, remaining = sum([loads[i] for i in free]), rest
        for i in free:
            more = min(bound - given[i], max(1, remaining * loads[i] // mass), rest)
            given[i] = given[i] + more
            rest = rest - more
    return np.array(given)


def normal_values(key, shape, scale, bound, cuts=(), held_as=jnp.bfloat16):
    drawn = scale * jax.random.normal(key, shape, jnp.float32)
    if cuts:
        drawn = drawn * levels(key, shape, cuts, -0.22, 0.18)
    return jnp.clip(drawn, -bound, bound).astype(held_as)


def setup_inputs(seed: int = 0) -> dict:
    key_of = jax.random.split(jax.random.key(seed), 14)
    queries = draw_queries(jax.random.fold_in(key_of[13], 71), 0)
    span_keys = draw_span_keys(jax.random.fold_in(key_of[13], 71), 0)
    span_values = normal_values(key_of[2], (REQS, SPAN, KV_HEADS * HEAD_DIM), 1.0, 6.0, ((0, 4), (1, 8)))
    cache_keys = normal_values(key_of[3], (REQS, CTX, KV_HEADS * HEAD_DIM), 1.0, 6.0, ((0, 4), (1, 8)))
    cache_values = normal_values(key_of[4], (REQS, CTX, KV_HEADS * HEAD_DIM), 1.0, 6.0, ((0, 4), (1, 8)))
    lengths = ragged(key_of[5], REQS, 2 * CTX + CTX // 2, CTX, 2).astype(jnp.int32)
    inputs = normal_values(key_of[6], (REQS, SPAN, D), 0.1, 0.59765625, ((0, 4), (1, 8)))
    w_out = normal_values(key_of[7], (HEADS * HEAD_DIM, D), (HEADS * HEAD_DIM) ** -0.5, 0.125)
    norm_gain = jnp.clip(1.0 + 0.18 * jax.random.normal(key_of[8], (D,), jnp.float32), 0.1, 1.9)
    route_ids_keys = jax.random.split(jax.random.fold_in(key_of[9], 1), REQS * SPAN // TOK_DEV)
    route_ids_turns = jax.random.permutation(jax.random.fold_in(key_of[9], 3), REQS * SPAN // TOK_DEV)
    route_ids = jax.vmap(lambda own, number: routed_block(jax.random.fold_in(key_of[9], 2), own, number, TOK_DEV, EXPERTS, TOP, CAP, 2))(route_ids_keys, route_ids_turns).reshape((REQS, SPAN, TOP))
    route_weights = jnp.clip(0.2 + 0.8 * jax.random.uniform(key_of[10], (REQS, SPAN, TOP), jnp.float32) ** levels(key_of[10], (REQS, SPAN, TOP), ((0, 4), (1, 8)), -0.2, 0.2), 0.2, 1.0)
    w_gate_up = normal_values(key_of[11], (2 * EXPERTS, 2 * HALF, D), D ** -0.5, 0.125, ((0, 32),))
    w_down = normal_values(key_of[12], (2 * EXPERTS, HALF, D), FF_E ** -0.5, 0.15625, ((0, 32),))
    return dict(queries=queries, span_keys=span_keys, span_values=span_values, cache_keys=cache_keys, cache_values=cache_values, lengths=lengths, inputs=inputs, w_out=w_out, norm_gain=norm_gain, route_ids=route_ids, route_weights=route_weights, w_gate_up=w_gate_up, w_down=w_down)


def attend_request(query_rows, key_rows, value_rows, length):
    group_size = HEADS // KV_HEADS
    keys_wide = key_rows.astype(jnp.float32).reshape(-1, KV_HEADS, HEAD_DIM)
    values_wide = value_rows.astype(jnp.float32).reshape(-1, KV_HEADS, HEAD_DIM)
    key_index = jnp.arange(key_rows.shape[0], dtype=jnp.int32)
    block_size = min(256, SPAN)
    starts = jnp.arange(SPAN // block_size, dtype=jnp.int32) * block_size

    def one_block(first_row):
        picked = lax.dynamic_slice_in_dim(query_rows, first_row, block_size, 0)
        picked = picked.astype(jnp.float32).reshape(block_size, KV_HEADS, group_size, HEAD_DIM)
        scores = jnp.einsum('qgrd,kgd->qgrk', picked, keys_wide) / math.sqrt(HEAD_DIM)
        row_index = first_row + jnp.arange(block_size, dtype=jnp.int32)
        in_cache = (key_index < CTX) & (key_index < length)
        in_span = (key_index >= CTX) & (key_index - CTX <= row_index[:, None])
        visible = (in_cache[None, :] | in_span)[:, None, None, :]
        masked = jnp.where(visible, scores, -1e+30)
        row_peak = lax.optimization_barrier(jnp.max(masked, axis=-1, keepdims=True))
        probs_now = jnp.where(visible, jnp.exp(masked - row_peak), 0.0)
        row_total = lax.optimization_barrier(jnp.sum(probs_now, axis=-1))
        rounded = lax.optimization_barrier(probs_now.astype(jnp.bfloat16)).astype(jnp.float32)
        mixed_rows = jnp.einsum('qgrk,kgd->qgrd', rounded, values_wide) / row_total[..., None]
        return mixed_rows.reshape(block_size, HEADS * HEAD_DIM).astype(jnp.bfloat16)
    return lax.map(one_block, starts).reshape(SPAN, HEADS * HEAD_DIM)

def reference(queries, span_keys, span_values, cache_keys, cache_values, lengths, inputs, w_out, norm_gain, route_ids, route_weights, w_gate_up, w_down):
    attended = jnp.stack([attend_request(queries[request], jnp.concatenate([cache_keys[request], span_keys[request]], 0), jnp.concatenate([cache_values[request], span_values[request]], 0), lengths[request]) for request in range(REQS)])
    token_count = REQS * SPAN
    residual = inputs.reshape(token_count, D).astype(jnp.float32) + jnp.dot(attended.reshape(token_count, HEADS * HEAD_DIM), w_out, preferred_element_type=jnp.float32)
    normalized = (residual * lax.rsqrt(lax.optimization_barrier(jnp.mean(residual * residual, axis=-1, keepdims=True)) + 1e-06) * norm_gain).astype(jnp.bfloat16)
    tok_dev = SPAN // N_BLK
    blocks = token_count // tok_dev
    expert_ids = route_ids.reshape(blocks, tok_dev * TOP)
    onehot = (expert_ids[..., None] == jnp.arange(EXPERTS, dtype=jnp.int32)).astype(jnp.int32)
    earlier = jnp.cumsum(onehot, axis=1) - onehot
    slot_index = lax.optimization_barrier(jnp.sum(earlier * onehot, axis=-1))
    token_of = (jnp.arange(token_count * TOP, dtype=jnp.int32) // TOP).reshape(blocks, -1)
    block_of = jnp.broadcast_to(jnp.arange(blocks, dtype=jnp.int32)[:, None], expert_ids.shape)
    slot_table = jnp.full((EXPERTS, blocks, CAP), token_count, jnp.int32).at[expert_ids, block_of, slot_index].set(token_of)
    scale_table = jnp.zeros((EXPERTS, blocks, CAP), jnp.float32).at[expert_ids, block_of, slot_index].set(route_weights.reshape(blocks, -1).astype(jnp.float32))
    padded = jnp.concatenate([normalized, jnp.zeros((1, D), jnp.bfloat16)], 0)

    def one_expert(running, expert):
        rows_index = lax.dynamic_index_in_dim(slot_table, expert, 0, keepdims=False).reshape(-1)
        picked = padded[rows_index]
        summed = jnp.zeros((picked.shape[0], D), jnp.float32)
        for half_index in range(2):
            gate_up = lax.dynamic_index_in_dim(w_gate_up, 2 * expert + half_index, 0, keepdims=False)
            hidden = jnp.dot(picked, gate_up.T, preferred_element_type=jnp.float32)
            activated = (jax.nn.silu(hidden[:, :HALF]) * hidden[:, HALF:]).astype(jnp.bfloat16)
            down_rows = lax.dynamic_index_in_dim(w_down, 2 * expert + half_index, 0, keepdims=False)
            partial_value = jnp.dot(activated, down_rows, preferred_element_type=jnp.float32)
            summed = summed + lax.optimization_barrier(partial_value.astype(jnp.bfloat16)).astype(jnp.float32)
        factor = lax.dynamic_index_in_dim(scale_table, expert, 0, keepdims=False).reshape(-1)
        running = running.at[rows_index].add(factor[:, None] * summed, mode='drop')
        return (running, None)
    expert_sum, _ = lax.scan(one_expert, jnp.zeros((token_count, D), jnp.float32), jnp.arange(EXPERTS, dtype=jnp.int32))
    return (residual + expert_sum).astype(jnp.bfloat16).reshape(REQS, SPAN, D)
```

```python
import math

import jax
import jax.numpy as jnp
from jax import lax
from jax.experimental import pallas as pl
from jax.experimental.pallas import tpu as pltpu
from jax.sharding import PartitionSpec as P

D = 2048
HEADS = 16
KV_HEADS = 4
HEAD_DIM = 128
EXPERTS = 64
TOP = 6
NEG = -1e30
LOG2E_SCALE = 1.4426950408889634 / math.sqrt(HEAD_DIM)


def attend_kernel(sub, n_sub, scal, q_ref, ck_ref, cv_ref, sk_ref, sv_ref, o_ref, cvx, svx, acc, peak):
    step = pl.program_id(0)
    length, part = scal[0], scal[1]
    n_src, cl, _ = ck_ref.shape
    tok = sk_ref.shape[1]
    rows = q_ref.shape[1]
    tile = rows // n_sub

    @pl.when(step == 0)
    def _():
        cvx[:, :, :HEAD_DIM] = cv_ref[...]
        cvx[:, :, HEAD_DIM:] = jnp.ones((n_src, cl, HEAD_DIM), jnp.bfloat16)
        svx[:, :, :HEAD_DIM] = sv_ref[...]
        svx[:, :, HEAD_DIM:] = jnp.ones((n_src, tok, HEAD_DIM), jnp.bfloat16)

    acc[...] = jnp.zeros_like(acc)
    peak[...] = jnp.full_like(peak, NEG)

    def chunk(keys, vals, mask_of):
        for piece in range(n_sub):
            at = pl.ds(piece * tile, tile)
            s = lax.dot_general(
                q_ref[0, at, :], keys, (((1,), (1,)), ((), ())), preferred_element_type=jnp.float32
            )
            if mask_of is not None:
                s = jnp.where(mask_of(s.shape, piece * tile), s, NEG)
            old = peak[at, :]
            new = jnp.maximum(old, jnp.max(s, axis=1, keepdims=True))
            p = jnp.exp2((s - new[:, :1]) * LOG2E_SCALE).astype(jnp.bfloat16)
            fade = jnp.exp2((old - new) * LOG2E_SCALE)
            acc[at, :] = acc[at, :] * jnp.concatenate([fade, fade], 1) + jnp.dot(
                p, vals, preferred_element_type=jnp.float32
            )
            peak[at, :] = new

    full = length // cl

    @pl.loop(0, full)
    def _(c):
        chunk(ck_ref[c], cvx[c], None)

    left = length - full * cl

    @pl.when(left > 0)
    def _():
        chunk(
            ck_ref[full],
            cvx[full],
            lambda shape, first: lax.broadcasted_iota(jnp.int32, shape, 1) < left,
        )

    @pl.loop(0, step)
    def _(c):
        chunk(sk_ref[c], svx[c], None)

    def causal(shape, first):
        row = lax.rem(first + lax.broadcasted_iota(jnp.int32, shape, 0), sub) + part * sub
        return lax.broadcasted_iota(jnp.int32, shape, 1) <= row

    chunk(sk_ref[step], svx[step], causal)
    o_ref[0] = (acc[:, :HEAD_DIM] / acc[:, HEAD_DIM:]).astype(jnp.bfloat16)


def attend(packed, scal, cl, tok, rows, sub):
    n_src = packed.shape[0]
    whole = lambda size, place: pl.BlockSpec((n_src, size, HEAD_DIM), lambda s: (0, place, 0))
    q_at = (2 * cl + 2 * tok) // rows
    n_sub = 2 if rows >= 256 else 1
    keys = n_src * (cl + tok)
    return pl.pallas_call(
        lambda *refs: attend_kernel(sub, n_sub, *refs),
        grid=(n_src,),
        out_shape=jax.ShapeDtypeStruct((n_src, rows, HEAD_DIM), jnp.bfloat16),
        in_specs=[
            pl.BlockSpec(memory_space=pltpu.SMEM),
            pl.BlockSpec((1, rows, HEAD_DIM), lambda s: (s, q_at, 0)),
            whole(cl, 0),
            whole(cl, 1),
            whole(tok, 2 * cl // tok),
            whole(tok, 2 * cl // tok + 1),
        ],
        out_specs=pl.BlockSpec((1, rows, HEAD_DIM), lambda s: (s, 0, 0)),
        scratch_shapes=[
            pltpu.VMEM((n_src, cl, 2 * HEAD_DIM), jnp.bfloat16),
            pltpu.VMEM((n_src, tok, 2 * HEAD_DIM), jnp.bfloat16),
            pltpu.VMEM((rows, 2 * HEAD_DIM), jnp.float32),
            pltpu.VMEM((rows, HEAD_DIM), jnp.float32),
        ],
        compiler_params=pltpu.CompilerParams(vmem_limit_bytes=40 * 1024 * 1024),
        cost_estimate=pl.CostEstimate(
            flops=4 * n_src * rows * keys * HEAD_DIM,
            bytes_accessed=2 * packed.size,
            transcendentals=n_src * rows * keys,
        ),
        name="attend",
    )(scal, packed, packed, packed, packed, packed)


def expert_kernel(x_ref, up_ref, down_ref, o_ref, acc):
    half = pl.program_id(1)
    n_src, _, cap, width = x_ref.shape
    hidden = down_ref.shape[1]
    x = x_ref[...].reshape(n_src * cap, width)
    dims = (((1,), (1,)), ((), ()))
    gate = lax.dot_general(x, up_ref[0, :hidden, :], dims, preferred_element_type=jnp.float32)
    up = lax.dot_general(x, up_ref[0, hidden:, :], dims, preferred_element_type=jnp.float32)
    activated = (gate / (1.0 + jnp.exp(-gate)) * up).astype(jnp.bfloat16)
    part = jnp.dot(activated, down_ref[0], preferred_element_type=jnp.float32)

    @pl.when(half == 0)
    def _():
        acc[...] = part

    @pl.when(half > 0)
    def _():
        acc[...] += part

    @pl.when(half == pl.num_programs(1) - 1)
    def _():
        o_ref[...] = acc[...].astype(jnp.bfloat16).reshape(n_src, 1, cap, width)


def run_experts(arrived, w_gate_up, w_down, halves):
    n_src, owned, cap, width = arrived.shape
    both, hidden = w_gate_up.shape[1], w_down.shape[1]
    rows = n_src * cap
    blk = pl.BlockSpec((n_src, 1, cap, width), lambda e, h: (0, e, 0, 0))
    return pl.pallas_call(
        expert_kernel,
        grid=(owned, halves),
        out_shape=jax.ShapeDtypeStruct(arrived.shape, jnp.bfloat16),
        in_specs=[
            blk,
            pl.BlockSpec((1, both, width), lambda e, h: (e * halves + h, 0, 0)),
            pl.BlockSpec((1, hidden, width), lambda e, h: (e * halves + h, 0, 0)),
        ],
        out_specs=blk,
        scratch_shapes=[pltpu.VMEM((rows, width), jnp.float32)],
        compiler_params=pltpu.CompilerParams(vmem_limit_bytes=56 * 1024 * 1024),
        cost_estimate=pl.CostEstimate(
            flops=6 * owned * halves * rows * width * hidden,
            bytes_accessed=2 * (w_gate_up.size + w_down.size + 2 * arrived.size),
            transcendentals=owned * halves * rows * hidden,
        ),
        name="experts",
    )(arrived, w_gate_up, w_down)


def local(
    queries,
    span_keys,
    span_values,
    cache_keys,
    cache_values,
    lengths,
    inputs,
    w_out,
    norm_gain,
    route_ids,
    route_weights,
    w_gate_up,
    w_down,
):
    tok = queries.shape[1]
    cl = cache_keys.shape[1]
    group = HEADS // KV_HEADS
    n_blk, n_req = lax.axis_size("blk"), lax.axis_size("req")
    my_blk, my_req = lax.axis_index("blk"), lax.axis_index("req")

    parts = n_blk // KV_HEADS
    sub = tok // parts

    def by_head(rows):
        split = rows.reshape(-1, KV_HEADS, HEAD_DIM).transpose(1, 0, 2)
        return jnp.broadcast_to(split[:, None], (KV_HEADS, parts) + split.shape[1:])

    q_pack = (
        queries[0]
        .reshape(parts, sub, KV_HEADS, group, HEAD_DIM)
        .transpose(2, 0, 3, 1, 4)
        .reshape(KV_HEADS, parts, group * sub, HEAD_DIM)
    )
    packed = jnp.concatenate(
        [
            by_head(cache_keys[0]),
            by_head(cache_values[0]),
            by_head(span_keys[0]),
            by_head(span_values[0]),
            q_pack,
        ],
        2,
    ).reshape(n_blk, -1, HEAD_DIM)
    packed = lax.all_to_all(packed, "blk", split_axis=0, concat_axis=0, tiled=True)
    scal = jnp.stack([lengths[0], lax.rem(my_blk, parts)]).astype(jnp.int32)
    mixed = attend(packed, scal, cl, tok, group * sub, sub)
    mixed = lax.all_to_all(mixed, "blk", split_axis=0, concat_axis=0, tiled=True)
    attended = (
        mixed.reshape(KV_HEADS, parts, group, sub, HEAD_DIM)
        .transpose(1, 3, 0, 2, 4)
        .reshape(tok, HEADS * HEAD_DIM)
    )

    residual = inputs[0].astype(jnp.float32) + jnp.dot(
        attended, w_out, preferred_element_type=jnp.float32
    )
    normalized = (
        residual
        * lax.rsqrt(jnp.mean(residual * residual, axis=-1, keepdims=True) + 1e-06)
        * norm_gain
    ).astype(jnp.bfloat16)

    per_device = 2 * EXPERTS // (n_req * n_blk)
    owned, halves = max(1, per_device // 2), min(2, per_device)
    copies = 2 // halves
    plane = EXPERTS // n_req
    cap = max(2, tok * TOP * 2 // EXPERTS)
    all_ids = lax.all_gather(route_ids[0], "req", axis=0)
    all_weights = lax.all_gather(route_weights[0], "req", axis=0)
    mine = my_req * plane + jnp.arange(plane, dtype=jnp.int32)
    named = all_ids[:, :, :, None] == mine
    chosen = jnp.any(named, axis=2)
    factor = jnp.sum(jnp.where(named, all_weights[..., None], 0.0), axis=2)
    earlier = jnp.tril(jnp.ones((tok, tok), jnp.bfloat16), -1)
    rank = jnp.einsum(
        "ts,zse->zte", earlier, chosen.astype(jnp.bfloat16), preferred_element_type=jnp.float32
    )
    slot = jnp.where(chosen, rank.astype(jnp.int32), -1)
    place = slot[..., None] == jnp.arange(cap, dtype=jnp.int32)
    send = place.astype(jnp.bfloat16)
    scale = jnp.where(place, factor[..., None], 0.0).astype(jnp.bfloat16)
    send = send.reshape(n_req, tok, plane * cap)
    scale = jnp.broadcast_to(
        scale[:, :, :, None, :], (n_req, tok, plane, copies, cap)
    ).reshape(n_req, tok, plane * copies * cap)

    shifts = [0] + sorted(range(1, n_req), key=lambda j: min(j, n_req - j))
    blocks = {0: normalized}
    for j in shifts[1:]:
        blocks[j] = lax.ppermute(
            normalized, "req", [(z, (z - j) % n_req) for z in range(n_req)]
        )
    total = residual
    for j in shifts:
        block = lax.rem(my_req + j, n_req)
        outgoing = lax.dot_general(
            lax.dynamic_index_in_dim(send, block, 0, keepdims=False),
            blocks[j],
            (((0,), (0,)), ((), ())),
            preferred_element_type=jnp.float32,
        ).astype(jnp.bfloat16)
        outgoing = jnp.broadcast_to(
            outgoing.reshape(plane, 1, cap, D), (plane, copies, cap, D)
        ).reshape(n_blk, owned * cap, D)
        arrived = lax.all_to_all(outgoing, "blk", split_axis=0, concat_axis=0, tiled=True)
        made = run_experts(arrived.reshape(n_blk, owned, cap, D), w_gate_up, w_down, halves)
        returned = lax.all_to_all(
            made.reshape(n_blk, owned * cap, D), "blk", split_axis=0, concat_axis=0, tiled=True
        )
        share = jnp.dot(
            lax.dynamic_index_in_dim(scale, block, 0, keepdims=False),
            returned.reshape(plane * copies * cap, D),
            preferred_element_type=jnp.float32,
        )
        if j:
            share = lax.ppermute(
                share.astype(jnp.bfloat16), "req", [(z, (z + j) % n_req) for z in range(n_req)]
            ).astype(jnp.float32)
        total = total + share
    return total.astype(jnp.bfloat16)[None]


def solution(mesh):
    in_specs = (
        P("req", "blk", None),
        P("req", "blk", None),
        P("req", "blk", None),
        P("req", "blk", None),
        P("req", "blk", None),
        P("req"),
        P("req", "blk", None),
        P(),
        P(),
        P("req", "blk", None),
        P("req", "blk", None),
        P(("req", "blk"), None, None),
        P(("req", "blk"), None, None),
    )
    out_specs = P("req", "blk", None)
    return jax.shard_map(local, mesh=mesh, in_specs=in_specs, out_specs=out_specs, check_vma=False)
```

```python
import math

import jax
import jax.numpy as jnp
from jax import lax
from jax.experimental import pallas as pl
from jax.experimental.pallas import tpu as pltpu
from jax.sharding import PartitionSpec as P

D = 2048
HEADS = 16
KV_HEADS = 4
HEAD_DIM = 128
EXPERTS = 64
TOP = 6
NEG = -1e30
LOG2E_SCALE = 1.4426950408889634 / math.sqrt(HEAD_DIM)


def attend_kernel(sub, n_sub, scal, q_ref, ck_ref, cv_ref, sk_ref, sv_ref, o_ref, cvx, svx, acc, peak):
    step = pl.program_id(0)
    length, part = scal[0], scal[1]
    n_src, cl, _ = ck_ref.shape
    tok = sk_ref.shape[1]
    rows = q_ref.shape[1]
    tile = rows // n_sub

    @pl.when(step == 0)
    def _():
        cvx[:, :, :HEAD_DIM] = cv_ref[...]
        cvx[:, :, HEAD_DIM:] = jnp.ones((n_src, cl, HEAD_DIM), jnp.bfloat16)
        svx[:, :, :HEAD_DIM] = sv_ref[...]
        svx[:, :, HEAD_DIM:] = jnp.ones((n_src, tok, HEAD_DIM), jnp.bfloat16)

    acc[...] = jnp.zeros_like(acc)
    peak[...] = jnp.full_like(peak, NEG)

    def chunk(keys, vals, mask_of):
        def score(piece):
            at = pl.ds(piece * tile, tile)
            return lax.dot_general(
                q_ref[0, at, :], keys, (((1,), (1,)), ((), ())), preferred_element_type=jnp.float32
            )

        ahead = score(0)
        for piece in range(n_sub):
            at = pl.ds(piece * tile, tile)
            s = ahead
            if piece + 1 < n_sub:
                ahead = score(piece + 1)
            if mask_of is not None:
                s = jnp.where(mask_of(s.shape, piece * tile), s, NEG)
            old = peak[at, :]
            new = jnp.maximum(old, jnp.max(s, axis=1, keepdims=True))
            p = jnp.exp2((s - new[:, :1]) * LOG2E_SCALE).astype(jnp.bfloat16)
            fade = jnp.exp2((old - new) * LOG2E_SCALE)
            acc[at, :] = acc[at, :] * jnp.concatenate([fade, fade], 1) + jnp.dot(
                p, vals, preferred_element_type=jnp.float32
            )
            peak[at, :] = new

    full = length // cl

    @pl.loop(0, full)
    def _(c):
        chunk(ck_ref[c], cvx[c], None)

    left = length - full * cl

    @pl.when(left > 0)
    def _():
        chunk(
            ck_ref[full],
            cvx[full],
            lambda shape, first: lax.broadcasted_iota(jnp.int32, shape, 1) < left,
        )

    @pl.loop(0, step)
    def _(c):
        chunk(sk_ref[c], svx[c], None)

    def causal(shape, first):
        row = lax.rem(first + lax.broadcasted_iota(jnp.int32, shape, 0), sub) + part * sub
        return lax.broadcasted_iota(jnp.int32, shape, 1) <= row

    chunk(sk_ref[step], svx[step], causal)
    o_ref[0] = (acc[:, :HEAD_DIM] / acc[:, HEAD_DIM:]).astype(jnp.bfloat16)


def attend(packed, scal, cl, tok, rows, sub):
    n_src = packed.shape[0]
    whole = lambda size, place: pl.BlockSpec((n_src, size, HEAD_DIM), lambda s: (0, place, 0))
    q_at = (2 * cl + 2 * tok) // rows
    n_sub = max(1, rows // 128)
    keys = n_src * (cl + tok)
    return pl.pallas_call(
        lambda *refs: attend_kernel(sub, n_sub, *refs),
        grid=(n_src,),
        out_shape=jax.ShapeDtypeStruct((n_src, rows, HEAD_DIM), jnp.bfloat16),
        in_specs=[
            pl.BlockSpec(memory_space=pltpu.SMEM),
            pl.BlockSpec((1, rows, HEAD_DIM), lambda s: (s, q_at, 0)),
            whole(cl, 0),
            whole(cl, 1),
            whole(tok, 2 * cl // tok),
            whole(tok, 2 * cl // tok + 1),
        ],
        out_specs=pl.BlockSpec((1, rows, HEAD_DIM), lambda s: (s, 0, 0)),
        scratch_shapes=[
            pltpu.VMEM((n_src, cl, 2 * HEAD_DIM), jnp.bfloat16),
            pltpu.VMEM((n_src, tok, 2 * HEAD_DIM), jnp.bfloat16),
            pltpu.VMEM((rows, 2 * HEAD_DIM), jnp.float32),
            pltpu.VMEM((rows, HEAD_DIM), jnp.float32),
        ],
        compiler_params=pltpu.CompilerParams(vmem_limit_bytes=40 * 1024 * 1024),
        cost_estimate=pl.CostEstimate(
            flops=4 * n_src * rows * keys * HEAD_DIM,
            bytes_accessed=2 * packed.size,
            transcendentals=n_src * rows * keys,
        ),
        name="attend",
    )(scal, packed, packed, packed, packed, packed)


def expert_kernel(x_ref, up_ref, down_ref, before, o_ref, turn_ref, acc):
    turn_ref[0] = 0
    half = pl.program_id(1)
    n_src, _, cap, width = x_ref.shape
    hidden = down_ref.shape[1]
    x = x_ref[...].reshape(n_src * cap, width)
    dims = (((1,), (1,)), ((), ()))
    gate = lax.dot_general(x, up_ref[0, :hidden, :], dims, preferred_element_type=jnp.float32)
    up = lax.dot_general(x, up_ref[0, hidden:, :], dims, preferred_element_type=jnp.float32)
    activated = (gate / (1.0 + jnp.exp(-gate)) * up).astype(jnp.bfloat16)
    part = jnp.dot(activated, down_ref[0], preferred_element_type=jnp.float32)

    @pl.when(half == 0)
    def _():
        acc[...] = part

    @pl.when(half > 0)
    def _():
        acc[...] += part

    @pl.when(half == pl.num_programs(1) - 1)
    def _():
        o_ref[...] = acc[...].astype(jnp.bfloat16).reshape(n_src, 1, cap, width)


def run_experts(arrived, w_gate_up, w_down, halves, before):
    n_src, owned, cap, width = arrived.shape
    both, hidden = w_gate_up.shape[1], w_down.shape[1]
    rows = n_src * cap
    blk = pl.BlockSpec((n_src, 1, cap, width), lambda e, h: (0, e, 0, 0))
    return pl.pallas_call(
        expert_kernel,
        grid=(owned, halves),
        out_shape=(
            jax.ShapeDtypeStruct(arrived.shape, jnp.bfloat16),
            jax.ShapeDtypeStruct((1,), jnp.int32),
        ),
        in_specs=[
            blk,
            pl.BlockSpec((1, both, width), lambda e, h: (e * halves + h, 0, 0)),
            pl.BlockSpec((1, hidden, width), lambda e, h: (e * halves + h, 0, 0)),
            pl.BlockSpec(memory_space=pl.ANY),
        ],
        out_specs=(blk, pl.BlockSpec(memory_space=pltpu.SMEM)),
        scratch_shapes=[pltpu.VMEM((rows, width), jnp.float32)],
        compiler_params=pltpu.CompilerParams(vmem_limit_bytes=56 * 1024 * 1024),
        cost_estimate=pl.CostEstimate(
            flops=6 * owned * halves * rows * width * hidden,
            bytes_accessed=2 * (w_gate_up.size + w_down.size + 2 * arrived.size),
            transcendentals=owned * halves * rows * hidden,
        ),
        name="experts",
    )(arrived, w_gate_up, w_down, before)


def local(
    queries,
    span_keys,
    span_values,
    cache_keys,
    cache_values,
    lengths,
    inputs,
    w_out,
    norm_gain,
    route_ids,
    route_weights,
    w_gate_up,
    w_down,
):
    tok = queries.shape[1]
    cl = cache_keys.shape[1]
    group = HEADS // KV_HEADS
    n_blk, n_req = lax.axis_size("blk"), lax.axis_size("req")
    my_blk, my_req = lax.axis_index("blk"), lax.axis_index("req")

    parts = n_blk // KV_HEADS
    sub = tok // parts

    def by_head(rows):
        split = rows.reshape(-1, KV_HEADS, HEAD_DIM).transpose(1, 0, 2)
        return jnp.broadcast_to(split[:, None], (KV_HEADS, parts) + split.shape[1:])

    q_pack = (
        queries[0]
        .reshape(parts, sub, KV_HEADS, group, HEAD_DIM)
        .transpose(2, 0, 3, 1, 4)
        .reshape(KV_HEADS, parts, group * sub, HEAD_DIM)
    )
    packed = jnp.concatenate(
        [
            by_head(cache_keys[0]),
            by_head(cache_values[0]),
            by_head(span_keys[0]),
            by_head(span_values[0]),
            q_pack,
        ],
        2,
    ).reshape(n_blk, -1, HEAD_DIM)
    packed = lax.all_to_all(packed, "blk", split_axis=0, concat_axis=0, tiled=True)
    scal = jnp.stack([lengths[0], lax.rem(my_blk, parts)]).astype(jnp.int32)
    mixed = attend(packed, scal, cl, tok, group * sub, sub)
    own_routes = jnp.concatenate([route_ids[0].T.astype(jnp.float32), route_weights[0].T], 0)
    routes = [own_routes] + [
        lax.ppermute(own_routes, "req", [(z, (z - j) % n_req) for z in range(n_req)])
        for j in range(1, n_req)
    ]
    mixed, routes = lax.optimization_barrier((mixed, jnp.stack(routes)))
    mixed = lax.all_to_all(mixed, "blk", split_axis=0, concat_axis=0, tiled=True)
    attended = (
        mixed.reshape(KV_HEADS, parts, group, sub, HEAD_DIM)
        .transpose(1, 3, 0, 2, 4)
        .reshape(tok, HEADS * HEAD_DIM)
    )

    residual = inputs[0].astype(jnp.float32) + jnp.dot(
        attended, w_out, preferred_element_type=jnp.float32
    )
    normalized = (
        residual
        * lax.rsqrt(jnp.mean(residual * residual, axis=-1, keepdims=True) + 1e-06)
        * norm_gain
    ).astype(jnp.bfloat16)

    per_device = 2 * EXPERTS // (n_req * n_blk)
    owned, halves = max(1, per_device // 2), min(2, per_device)
    copies = 2 // halves
    plane = EXPERTS // n_req
    cap = max(2, tok * TOP * 2 // EXPERTS)
    mine = (my_req * plane + jnp.arange(plane, dtype=jnp.int32)).astype(jnp.float32)
    named = routes[:, :TOP, :, None] == mine
    chosen = jnp.any(named, axis=1)
    factor = jnp.sum(jnp.where(named, routes[:, TOP:, :, None], 0.0), axis=1)
    earlier = jnp.tril(jnp.ones((tok, tok), jnp.bfloat16), -1)
    rank = jnp.einsum(
        "ts,zse->zte", earlier, chosen.astype(jnp.bfloat16), preferred_element_type=jnp.float32
    )
    slot = jnp.where(chosen, rank.astype(jnp.int32), -1)
    place = slot[..., None] == jnp.arange(cap, dtype=jnp.int32)
    send = place.astype(jnp.bfloat16)
    scale = jnp.where(place, factor[..., None], 0.0).astype(jnp.bfloat16)
    send = send.reshape(n_req, tok, plane * cap)
    scale = jnp.broadcast_to(
        scale[:, :, :, None, :], (n_req, tok, plane, copies, cap)
    ).reshape(n_req, tok, plane * copies * cap)

    blocks = [normalized] + [
        lax.ppermute(normalized, "req", [(z, (z - j) % n_req) for z in range(n_req)])
        for j in range(1, n_req)
    ]
    total = residual
    turns, shares = [], []
    for j in range(n_req):
        picks = send[j]
        if j:
            picks = lax.dynamic_index_in_dim(send, j + turns[max(0, j - 2)][0], 0, keepdims=False)
        outgoing = lax.dot_general(
            picks,
            blocks[j],
            (((0,), (0,)), ((), ())),
            preferred_element_type=jnp.float32,
        ).astype(jnp.bfloat16)
        outgoing = jnp.broadcast_to(
            outgoing.reshape(plane, 1, cap, D), (plane, copies, cap, D)
        ).reshape(n_blk, owned * cap, D)
        arrived = lax.all_to_all(outgoing, "blk", split_axis=0, concat_axis=0, tiled=True)
        made, turn = run_experts(
            arrived.reshape(n_blk, owned, cap, D),
            w_gate_up,
            w_down,
            halves,
            shares[j - 2] if j >= 2 else own_routes,
        )
        turns.append(turn)
        returned = lax.all_to_all(
            made.reshape(n_blk, owned * cap, D), "blk", split_axis=0, concat_axis=0, tiled=True
        )
        share = jnp.dot(
            scale[j],
            returned.reshape(plane * copies * cap, D),
            preferred_element_type=jnp.float32,
        )
        if j:
            share = share.astype(jnp.bfloat16)
        shares.append(share)
        if j:
            share = lax.ppermute(
                share, "req", [(z, (z + j) % n_req) for z in range(n_req)]
            ).astype(jnp.float32)
        total = total + share
    return total.astype(jnp.bfloat16)[None]


def solution(mesh):
    in_specs = (
        P("req", "blk", None),
        P("req", "blk", None),
        P("req", "blk", None),
        P("req", "blk", None),
        P("req", "blk", None),
        P("req"),
        P("req", "blk", None),
        P(),
        P(),
        P("req", "blk", None),
        P("req", "blk", None),
        P(("req", "blk"), None, None),
        P(("req", "blk"), None, None),
    )
    out_specs = P("req", "blk", None)
    return jax.shard_map(local, mesh=mesh, in_specs=in_specs, out_specs=out_specs, check_vma=False)
```
